512 devices in a mesh: frames: 16 (over z_lo, x, core), heads: 32 (over z_hi, y).
Axes of the slice: x: 4, y: 8, z: 8 (z_hi: 4, z_lo: 2; z = z_hi * 2 + z_lo), core: 2. Of those that a mesh axis runs over, the one named last changes fastest.
Arguments:
- queries: bfloat16 [4096, 4096], P('frames', 'heads'), may hold values from -6 to 6
- local_keys: bfloat16 [4096, 4096], P('frames', 'heads'), may hold values from -6 to 6
- local_values: bfloat16 [4096, 4096], P('frames', 'heads'), may hold values from -6 to 6
- cache_keys: bfloat16 [32, 512, 4096], P('frames', None, 'heads'), may hold values from -6 to 6
- cache_values: bfloat16 [32, 512, 4096], P('frames', None, 'heads'), may hold values from -6 to 6
- windows: int32 [16, 4], replicated, may hold values from 0 to 31, as said below
- counts: int32 [16], replicated, may hold values from 1 to 4, as said below
- slot_of: int32 [32], replicated, may hold values from 0 to 31, as said below
- residual: bfloat16 [5120, 4096], P('heads', 'frames'), may hold values from -6 to 6
- out_weight: bfloat16 [5120, 4096], P('heads'), may hold values from -0.09375 to 0.09375
- gate_table: float32 [50, 5120], P(None, 'heads'), may hold values from -4 to 4
- timestep: int32 [1], replicated, may hold values from 0 to 49
Outputs:
- updated: bfloat16 [5120, 4096], P('heads', 'frames')
The draws below stay inside these ranges and needn't reach their ends.
Inputs may be any that keep to these rules, and one draw needn't show every extreme that they name: slot_of is a permutation of the storage rows. `windows`: within a row, the listed frames are stored on different indices of frames: the values slot_of[c] // 2 differ. `counts`: some query block has exactly 4 live entries.
All inputs are finite; a program needn't handle non-finite values.
Results may differ from the reference program's by a relative error of at most 0.01.
Values may be sent and summed in bfloat16 or wider, within the bound.
A program may use at most 64 MiB of HBM per device.

```python
import jax
import jax.numpy as jnp
from jax import lax

D = 5120
HEAD = 128
HEADS = 32
TOK_DEV = 256
FRAME_TOK = 512
FRAMES_DEV = 2
W_MOST = 4
STEPS = 50
BLOCKS = 16
TOKENS = 4096
CACHED = 32


def storage_order(key):
    return jax.random.permutation(jax.random.fold_in(key, 29), CACHED).astype(jnp.int32)


def draw_queries(key, part):
    key = jax.random.fold_in(key, 11)
    first = jax.random.fold_in(key, 0)
    values = jnp.clip(2.0 * jax.random.normal(first, (TOKENS, HEADS * HEAD), jnp.float32), -6.0, 6.0)
    return values.astype(jnp.bfloat16)


def draw_cache_keys(key, part):
    key = jax.random.fold_in(key, 13)
    shape = (CACHED, FRAME_TOK, HEADS * HEAD)
    values = jnp.clip(jax.random.normal(key, shape, jnp.float32), -6.0, 6.0)
    return values.astype(jnp.bfloat16)


def draw_slot_of(key, part):
    order = storage_order(key)
    return order


def draw_windows(key, part):
    order = storage_order(key)
    frame_of_slot = jnp.argsort(order, stable=True).astype(jnp.int32)
    key = jax.random.fold_in(key, 5)
    block_keys = jax.random.split(key, BLOCKS)
    holder_total = CACHED // FRAMES_DEV

    def pick_frames(block_key):
        first, second = jax.random.split(block_key)
        holders = jax.random.permutation(first, holder_total)[:W_MOST].astype(jnp.int32)
        within = jax.random.randint(second, (W_MOST,), 0, FRAMES_DEV).astype(jnp.int32)
        return frame_of_slot[holders * FRAMES_DEV + within]
    return jax.vmap(pick_frames)(block_keys).astype(jnp.int32)


def draw_counts(key, part):
    key = jax.random.fold_in(key, 7)
    first, second = jax.random.split(key)
    lengths = jax.random.randint(first, (BLOCKS,), 1, W_MOST // 2 + 1)
    fullest = jax.random.randint(second, (), 0, BLOCKS)
    return jnp.where(jnp.arange(BLOCKS) == fullest, W_MOST, lengths).astype(jnp.int32)


def level_of(key, dims, shards, least, top_value):
    gain, own = 1.0, jax.random.fold_in(key, 6)
    for dim, blocks in shards:
        heights = jnp.exp(jax.random.uniform(jax.random.fold_in(own, dim), (blocks,), jnp.float32, least / len(shards), top_value / len(shards)))
        gain = gain * jnp.repeat(heights, dims[dim] // blocks).reshape([-1 if axis == dim else 1 for axis in range(len(dims))])
    return gain


def gaussian(stream_key, extent, deviation, bound, shards=(), kind=jnp.bfloat16):
    values = deviation * jax.random.normal(stream_key, extent, jnp.float32)
    if shards:
        values = values * level_of(stream_key, extent, shards, -0.22, 0.18)
    return jnp.clip(values, -bound, bound).astype(kind)


def setup_inputs(seed: int = 0) -> dict:
    keys = jax.random.split(jax.random.key(seed), 13)
    return {
        "queries": draw_queries(jax.random.fold_in(keys[12], 71), 0),
        "local_keys": gaussian(keys[1], (TOKENS, HEADS * HEAD), 1.0, 6.0, ((0, 16), (1, 32))),
        "local_values": gaussian(keys[2], (TOKENS, HEADS * HEAD), 1.0, 6.0, ((0, 16), (1, 32))),
        "cache_keys": draw_cache_keys(jax.random.fold_in(keys[12], 71), 0),
        "cache_values": gaussian(keys[4], (CACHED, FRAME_TOK, HEADS * HEAD), 1.0, 6.0, ((0, 16), (2, 32))),
        "windows": draw_windows(jax.random.fold_in(keys[12], 71), 0),
        "counts": draw_counts(jax.random.fold_in(keys[12], 71), 0),
        "slot_of": draw_slot_of(jax.random.fold_in(keys[12], 71), 0),
        "residual": gaussian(keys[8], (D, TOKENS), 1.0, 6.0, ((0, 32), (1, 16))),
        "out_weight": gaussian(keys[9], (D, HEADS * HEAD), (HEADS * HEAD) ** -0.5, 0.09375, ((0, 32),)),
        "gate_table": gaussian(keys[10], (STEPS, D), 1.0, 4.0, ((1, 32),), jnp.float32),
        "timestep": jax.random.randint(keys[11], (1,), 0, STEPS).astype(jnp.int32),
    }


def block_attention(block_queries, block_keys, block_values, live_keys):
    queries_f = block_queries.astype(jnp.float32).reshape(-1, HEADS, HEAD)
    keys_f = block_keys.astype(jnp.float32).reshape(-1, HEADS, HEAD)
    values_f = block_values.astype(jnp.float32).reshape(-1, HEADS, HEAD)
    scores = jnp.einsum("thd,khd->htk", queries_f, keys_f) * (HEAD ** -0.5)
    scores = jnp.where(live_keys[None, None, :], scores, -jnp.inf)
    row_top = jnp.max(scores, axis=2, keepdims=True)
    raised = jnp.exp(scores - row_top)
    denom_sum = jnp.sum(raised, axis=2)
    rounded = lax.optimization_barrier(raised.astype(jnp.bfloat16))
    weighted = jnp.einsum("htk,khd->thd", rounded.astype(jnp.float32), values_f)
    return weighted / jnp.transpose(denom_sum)[:, :, None]


def reference(queries, local_keys, local_values, cache_keys, cache_values, windows, counts, slot_of, residual, out_weight, gate_table, timestep):
    width = HEADS * HEAD

    def one_block(block_id):
        start = block_id * TOK_DEV
        block_queries = lax.dynamic_slice_in_dim(queries, start, TOK_DEV, 0)
        own_keys = lax.dynamic_slice_in_dim(local_keys, start, TOK_DEV, 0)
        own_values = lax.dynamic_slice_in_dim(local_values, start, TOK_DEV, 0)
        frame_ids = windows[block_id]
        slot_ids = slot_of[frame_ids]
        far_keys = cache_keys[slot_ids].reshape(W_MOST * FRAME_TOK, width)
        far_values = cache_values[slot_ids].reshape(W_MOST * FRAME_TOK, width)
        live_far = jnp.repeat(jnp.arange(W_MOST, dtype=jnp.int32) < counts[block_id], FRAME_TOK)
        live_own = jnp.arange(TOK_DEV, dtype=jnp.int32) >= 0
        live_keys = jnp.concatenate([live_own, live_far])
        all_keys = jnp.concatenate([own_keys, far_keys], axis=0)
        all_values = jnp.concatenate([own_values, far_values], axis=0)
        return block_attention(block_queries, all_keys, all_values, live_keys)

    blocks_out = lax.map(one_block, jnp.arange(BLOCKS, dtype=jnp.int32))
    attended = blocks_out.reshape(TOKENS, width).astype(jnp.bfloat16)
    mixed = jnp.dot(out_weight, jnp.transpose(attended), preferred_element_type=jnp.float32)
    gate_row = gate_table[timestep[0]]
    return (residual.astype(jnp.float32) + gate_row[:, None] * mixed).astype(jnp.bfloat16)
```

```python
import functools

import jax
import jax.numpy as jnp
from jax import lax
from jax.experimental import pallas as pl
from jax.experimental.pallas import tpu as pltpu
from jax.sharding import PartitionSpec as P

MESH = pl.DeviceIdType.MESH
BF = jnp.bfloat16
F32 = jnp.float32
NX, NZL, NC, NZH, NY = 4, 2, 2, 4, 8
GROUP = NX * NZL
HEAD = 128
TOK = 256
FRAME = 512
FEAT = 160
HALF_FEAT = FEAT // 2
COLS = NY * HEAD
MSG = HEAD + 16
NEG = -(2.0**100)
SCALE2 = HEAD ** (-0.5) * 1.4426950408889634


def coords():
    f = lax.axis_index("frames")
    h = lax.axis_index("heads")
    return f // 8, (f // 2) % 4, f % 2, h // 8, h % 8


def device(zl, x, c, zh, y):
    return (zl * 8 + x * 2 + c, zh * 8 + y)


def kernel(
    splits,
    q_hbm, lk_hbm, lv_hbm, ck_hbm, cv_hbm, windows, counts, slot_of, res_hbm, w_hbm, gate_hbm, step,
    out_ref,
    qall, kbuf, vbuf, vt, lk, lv, lvt, sent, came, acc, top, den, att, wg, part, parts_in, resid, gate, gcol,
    sem_load, sem_kv_s, sem_kv_r, sem_q_s, sem_q_r, sem_p_s, sem_p_r,
    sem_a_s, sem_a_r, sem_w_s, sem_w_r, sem_f_s, sem_f_r, sem_m_s, sem_m_r,
):
    zl, x, c, zh, y = coords()
    width = TOK // splits

    def frame_peer(o, sign):
        dz, dx = o // NX, o % NX
        return device((zl + dz) % NZL, (x + sign * dx + NX) % NX, c, zh, y)

    def y_peer(k):
        return device(zl, x, c, zh, (y + k) % NY)

    def z_peer(k):
        return device(zl, x, c, (zh + k) % NZH, y)

    other_core = device(zl, x, 1 - c, zh, y)

    mine = pl.ds(pl.multiple_of(c * 2, 2), 2)
    loads = [
        pltpu.make_async_copy(ck_hbm, kbuf.at[mine], sem_load.at[0]),
        pltpu.make_async_copy(cv_hbm, vbuf.at[mine], sem_load.at[1]),
        pltpu.make_async_copy(q_hbm, qall.at[0], sem_load.at[2]),
        pltpu.make_async_copy(lk_hbm, lk, sem_load.at[3]),
        pltpu.make_async_copy(lv_hbm, lv, sem_load.at[4]),
        pltpu.make_async_copy(gate_hbm, gate, sem_load.at[5]),
        pltpu.make_async_copy(res_hbm, resid, sem_load.at[6]),
        pltpu.make_async_copy(
            w_hbm.at[:, pl.ds(pl.multiple_of(zh * COLS, COLS), COLS)], wg.at[zh], sem_load.at[7]
        ),
    ]
    for load in loads:
        load.start()

    barrier = pltpu.get_barrier_semaphore()
    peers = [other_core]
    peers += [frame_peer(o, 1) for o in range(1, GROUP)]
    peers += [y_peer(k) for k in range(1, NY)]
    peers += [z_peer(k) for k in range(1, NZH)]
    for peer in peers:
        pl.semaphore_signal(barrier, inc=1, device_id=peer, device_id_type=MESH)
    pl.semaphore_wait(barrier, len(peers))

    def remote(src, dst, send, recv, peer):
        return pltpu.make_async_remote_copy(
            src_ref=src, dst_ref=dst, send_sem=send, recv_sem=recv, device_id=peer, device_id_type=MESH
        )

    def span(t):
        return pl.ds(t * width, width)

    kv = [
        remote(ck_hbm, kbuf.at[mine], sem_kv_s.at[0], sem_kv_r.at[0], other_core),
        remote(cv_hbm, vbuf.at[mine], sem_kv_s.at[1], sem_kv_r.at[1], other_core),
    ]

    def q_copy(t, o):
        return remote(
            q_hbm.at[span(t)], qall.at[o, span(t)], sem_q_s.at[t, o], sem_q_r.at[t, o], frame_peer(o, 1)
        )

    def p_copy(t, o):
        return remote(sent.at[t, o], came.at[t, o], sem_p_s.at[t, o], sem_p_r.at[t, o], frame_peer(o, -1))

    def a_copy(t, k):
        return remote(att.at[t, y], att.at[t, y], sem_a_s.at[t, k], sem_a_r.at[t, k], y_peer(k))

    rows = pl.ds(pl.multiple_of(c * HALF_FEAT, 16), HALF_FEAT)

    def w_copy(k):
        there = (zh + k) % NZH
        return remote(
            w_hbm.at[rows, pl.ds(pl.multiple_of(there * COLS, COLS), COLS)],
            wg.at[zh, rows], sem_w_s.at[k], sem_w_r.at[k], z_peer(k),
        )

    def f_copy(k):
        there = (zh + NZH - k) % NZH
        return remote(wg.at[there, rows], wg.at[there, rows], sem_f_s.at[k], sem_f_r.at[k], other_core)

    def m_copy(t, k):
        return remote(part.at[t, k], parts_in.at[t, k], sem_m_s.at[t, k], sem_m_r.at[t, k], z_peer(k))

    for copy in kv:
        copy.start()
    for t in range(splits):

        @pl.loop(1, GROUP)
        def _(o):
            q_copy(t, o).start()

    for k in range(1, NZH):
        w_copy(k).start()

    for load in loads:
        load.wait()
    lvt[...] = lv[...].T
    for i in range(2):
        vt[c * 2 + i] = vbuf[c * 2 + i].T
    hot = lax.broadcasted_iota(jnp.int32, gate.shape, 0) == step[0]
    gcol[...] = jnp.sum(jnp.where(hot, gate[...], 0.0).T, axis=1, keepdims=True)
    for copy in kv:
        copy.wait_recv()
    for i in range(2):
        vt[(1 - c) * 2 + i] = vbuf[(1 - c) * 2 + i].T

    def listed(block, holder):
        frame, live = 0, 0
        for j in range(4):
            slot = slot_of[windows[block, j]]
            hit = jnp.logical_and(j < counts[block], slot // 2 == holder).astype(jnp.int32)
            frame = frame + hit * (slot % 2)
            live = live + hit
        return frame, live

    def scores(keys, q):
        return lax.dot_general(keys, q, (((1,), (1,)), ((), ())), preferred_element_type=F32)

    def attend(t, o, own):
        q = qall[o, span(t)]
        dz, dx = o // NX, o % NX
        block = ((zl + dz) % NZL) * 8 + ((x - dx + NX) % NX) * 2 + c
        pieces = []
        tops = []
        for d in range(2):
            frame, live = listed(block, zl * 8 + x * 2 + d)
            s = scores(kbuf[2 * d + frame], q) * SCALE2
            on = jnp.full((1, width), live, jnp.int32) > 0
            tops.append(jnp.where(on, jnp.max(s, axis=0, keepdims=True), NEG))
            pieces.append((s, on, vt[2 * d + frame]))
        if own:
            s = scores(lk[...], q) * SCALE2
            tops.append(jnp.max(s, axis=0, keepdims=True))
            pieces.append((s, None, lvt[...]))
        m = functools.reduce(jnp.maximum, tops).astype(BF).astype(F32)
        total, result = 0.0, 0.0
        for s, on, values in pieces:
            shift = -m if on is None else jnp.where(on, -m, NEG)
            p = jnp.exp2(s + shift)
            total = total + jnp.sum(p, axis=0, keepdims=True)
            result = result + jnp.dot(values, p.astype(BF), preferred_element_type=F32)
        return m, total, result

    def attend_own(t):
        m, total, result = attend(t, 0, True)
        acc[t] = result
        top[t] = jnp.broadcast_to(m, (8, width))
        den[t] = jnp.broadcast_to(total, (8, width))

    def visit(t, first, last):

        @pl.loop(first, last)
        def _(o):
            q_copy(t, o).wait_recv()
            m, total, result = attend(t, o, False)
            sent[t, o, 0:HEAD] = result.astype(BF)
            high = total.astype(BF).astype(F32)
            row = lax.broadcasted_iota(jnp.int32, (16, width), 0)
            stats = jnp.where(row == 0, m, jnp.where(row == 1, high, total - high))
            sent[t, o, HEAD:MSG] = stats.astype(BF)
            p_copy(t, o).start()

    def merge(t):

        @pl.loop(1, GROUP)
        def _(o):
            p_copy(t, o).wait_recv()
            stats = came[t, o, HEAD:MSG].astype(F32)
            m = stats[0:1]
            total = stats[1:2] + stats[2:3]
            old = top[t, 0:1]
            new = jnp.maximum(old, m)
            keep = jnp.exp2(old - new)
            take = jnp.exp2(m - new)
            acc[t] = acc[t] * keep + came[t, o, 0:HEAD].astype(F32) * take
            den[t] = jnp.broadcast_to(den[t, 0:1] * keep + total * take, (8, width))
            top[t] = jnp.broadcast_to(new, (8, width))

        att[t, y] = (acc[t] / den[t, 0:1]).astype(BF)

        @pl.loop(1, NY)
        def _(k):
            a_copy(t, k).start()

    def project(t):

        @pl.loop(1, NY)
        def _(k):
            a_copy(t, k).wait_recv()

        rows_in = att[t].reshape(COLS, width)

        @pl.loop(1, NZH)
        def _(k):
            mixed = jnp.dot(wg[(zh + k) % NZH], rows_in, preferred_element_type=F32)
            part[t, k] = mixed.astype(BF)
            m_copy(t, k).start()

        return jnp.dot(wg[zh], rows_in, preferred_element_type=F32)

    def finish(t, mixed):
        for k in range(1, NZH):
            m_copy(t, k).wait_recv()
            mixed = mixed + parts_in[t, k].astype(F32)
        out_ref[:, span(t)] = (resid[:, span(t)].astype(F32) + gcol[...] * mixed).astype(BF)

    attend_own(0)
    visit(0, 1, GROUP)
    for t in range(1, splits):
        attend_own(t)
        visit(t, 1, GROUP // 2)
        merge(t - 1)
        visit(t, GROUP // 2, GROUP)
    merge(splits - 1)
    for k in range(1, NZH):
        w_copy(k).wait_recv()
        f_copy(k).start()
    for k in range(1, NZH):
        f_copy(k).wait_recv()
    own_parts = [project(t) for t in range(splits)]
    for t in range(splits):
        finish(t, own_parts[t])

    for copy in kv:
        copy.wait_send()
    for t in range(splits):

        @pl.loop(1, GROUP)
        def _(o):
            q_copy(t, o).wait_send()
            p_copy(t, o).wait_send()

        @pl.loop(1, NY)
        def _(k):
            a_copy(t, k).wait_send()

        for k in range(1, NZH):
            m_copy(t, k).wait_send()
    for k in range(1, NZH):
        w_copy(k).wait_send()
        f_copy(k).wait_send()


def local(splits, *args):
    width = TOK // splits
    anywhere = pl.BlockSpec(memory_space=pl.ANY)
    smem = pl.BlockSpec(memory_space=pltpu.SMEM)
    dma = pltpu.SemaphoreType.DMA
    return pl.pallas_call(
        functools.partial(kernel, splits),
        out_shape=jax.ShapeDtypeStruct((FEAT, TOK), BF),
        in_specs=[anywhere] * 5 + [smem] * 3 + [anywhere] * 3 + [smem],
        out_specs=pl.BlockSpec(memory_space=pltpu.VMEM),
        scratch_shapes=[
            pltpu.VMEM((GROUP, TOK, HEAD), BF),
            pltpu.VMEM((4, FRAME, HEAD), BF),
            pltpu.VMEM((4, FRAME, HEAD), BF),
            pltpu.VMEM((4, HEAD, FRAME), BF),
            pltpu.VMEM((TOK, HEAD), BF),
            pltpu.VMEM((TOK, HEAD), BF),
            pltpu.VMEM((HEAD, TOK), BF),
            pltpu.VMEM((splits, GROUP, MSG, width), BF),
            pltpu.VMEM((splits, GROUP, MSG, width), BF),
            pltpu.VMEM((splits, HEAD, width), F32),
            pltpu.VMEM((splits, 8, width), F32),
            pltpu.VMEM((splits, 8, width), F32),
            pltpu.VMEM((splits, NY, HEAD, width), BF),
            pltpu.VMEM((NZH, FEAT, COLS), BF),
            pltpu.VMEM((splits, NZH, FEAT, width), BF),
            pltpu.VMEM((splits, NZH, FEAT, width), BF),
            pltpu.VMEM((FEAT, TOK), BF),
            pltpu.VMEM((50, FEAT), F32),
            pltpu.VMEM((FEAT, 1), F32),
            dma((8,)),
            dma((2,)), dma((2,)),
            dma((splits, GROUP)), dma((splits, GROUP)),
            dma((splits, GROUP)), dma((splits, GROUP)),
            dma((splits, NY)), dma((splits, NY)),
            dma((NZH,)), dma((NZH,)),
            dma((NZH,)), dma((NZH,)),
            dma((splits, NZH)), dma((splits, NZH)),
        ],
        compiler_params=pltpu.CompilerParams(
            collective_id=0, has_side_effects=True, vmem_limit_bytes=32 << 20
        ),
        name="block_attention_projection",
    )(*args)


def solution(mesh):
    return jax.shard_map(
        functools.partial(local, 1),
        mesh=mesh,
        in_specs=(
            P("frames", "heads"),
            P("frames", "heads"),
            P("frames", "heads"),
            P("frames", None, "heads"),
            P("frames", None, "heads"),
            P(),
            P(),
            P(),
            P("heads", "frames"),
            P("heads", None),
            P(None, "heads"),
            P(),
        ),
        out_specs=P("heads", "frames"),
        check_vma=False,
    )
```

```python
import functools

import jax
import jax.numpy as jnp
from jax import lax
from jax.experimental import pallas as pl
from jax.experimental.pallas import tpu as pltpu
from jax.sharding import PartitionSpec as P

MESH = pl.DeviceIdType.MESH
BF = jnp.bfloat16
F32 = jnp.float32
NX, NZL, NC, NZH, NY = 4, 2, 2, 4, 8
GROUP = NX * NZL
HEAD = 128
TOK = 256
FRAME = 512
FEAT = 160
HALF_FEAT = FEAT // 2
COLS = 8 * HEAD
MSG = HEAD + 16
NEG = -(2.0**100)
SCALE2 = HEAD ** (-0.5) * 1.4426950408889634


def coords():
    f = lax.axis_index("frames")
    h = lax.axis_index("heads")
    return f // 8, (f // 2) % 4, f % 2, h // 8, h % 8


def device(zl, x, c, zh, y):
    return (zl * 8 + x * 2 + c, zh * 8 + y)


def kernel(
    splits,
    q_hbm, lk_hbm, lv_hbm, ck_hbm, cv_hbm, windows, counts, slot_of, res_hbm, w_hbm, gate_hbm, step,
    out_ref,
    qall, kbuf, vbuf, vt, lk, lv, lvt, sent, came, acc, top, den, att, wg, part, parts_in, resid, gate, gcol,
    sem_load, sem_kv_s, sem_kv_r, sem_q_s, sem_q_r, sem_p_s, sem_p_r,
    sem_a_s, sem_a_r, sem_w_s, sem_w_r, sem_f_s, sem_f_r, sem_m_s, sem_m_r,
):
    zl, x, c, zh, y = coords()
    width = TOK // splits

    def frame_peer(o, sign):
        dz, dx = o // NX, o % NX
        return device((zl + dz) % NZL, (x + sign * dx + NX) % NX, c, zh, y)

    pair, side = y // 2, y % 2

    def set_peer(k):
        return device(zl, x, c, (zh + k // 2) % NZH, 2 * pair + (side + k) % 2)

    def feature_peer(k):
        return device(zl, x, c, zh, (y + 2 * k) % NY)

    other_core = device(zl, x, 1 - c, zh, y)

    mine = pl.ds(pl.multiple_of(c * 2, 2), 2)
    loads = [
        pltpu.make_async_copy(ck_hbm, kbuf.at[mine], sem_load.at[0]),
        pltpu.make_async_copy(cv_hbm, vbuf.at[mine], sem_load.at[1]),
        pltpu.make_async_copy(q_hbm, qall.at[0], sem_load.at[2]),
        pltpu.make_async_copy(lk_hbm, lk, sem_load.at[3]),
        pltpu.make_async_copy(lv_hbm, lv, sem_load.at[4]),
        pltpu.make_async_copy(gate_hbm, gate, sem_load.at[5]),
        pltpu.make_async_copy(res_hbm, resid, sem_load.at[6]),
    ]
    for z in range(NZH):
        loads.append(
            pltpu.make_async_copy(
                w_hbm.at[:, pl.ds(pl.multiple_of(z * 1024 + pair * 256, 256), 256)],
                wg.at[pair, :, pl.ds(z * 256, 256)], sem_load.at[7 + z],
            )
        )
    for load in loads:
        load.start()

    barrier = pltpu.get_barrier_semaphore()
    peers = [other_core]
    peers += [frame_peer(o, 1) for o in range(1, GROUP)]
    peers += [set_peer(k) for k in range(1, 8)]
    peers += [feature_peer(k) for k in range(1, 4)]
    for peer in peers:
        pl.semaphore_signal(barrier, inc=1, device_id=peer, device_id_type=MESH)
    pl.semaphore_wait(barrier, len(peers))

    def remote(src, dst, send, recv, peer):
        return pltpu.make_async_remote_copy(
            src_ref=src, dst_ref=dst, send_sem=send, recv_sem=recv, device_id=peer, device_id_type=MESH
        )

    def span(t):
        return pl.ds(t * width, width)

    kv = [
        remote(ck_hbm, kbuf.at[mine], sem_kv_s.at[0], sem_kv_r.at[0], other_core),
        remote(cv_hbm, vbuf.at[mine], sem_kv_s.at[1], sem_kv_r.at[1], other_core),
    ]

    def q_copy(t, o):
        return remote(
            q_hbm.at[span(t)], qall.at[o, span(t)], sem_q_s.at[t, o], sem_q_r.at[t, o], frame_peer(o, 1)
        )

    def p_copy(t, o):
        return remote(sent.at[t, o], came.at[t, o], sem_p_s.at[t, o], sem_p_r.at[t, o], frame_peer(o, -1))

    def a_copy(t, k):
        here = att.at[t, 2 * zh + side]
        return remote(here, here, sem_a_s.at[t, k], sem_a_r.at[t, k], set_peer(k))

    rows = pl.ds(pl.multiple_of(c * HALF_FEAT, 16), HALF_FEAT)

    def w_copy(k, z):
        there = (pair + k) % 4
        return remote(
            w_hbm.at[rows, pl.ds(pl.multiple_of(z * 1024 + there * 256, 256), 256)],
            wg.at[pair, rows, pl.ds(z * 256, 256)], sem_w_s.at[k, z], sem_w_r.at[k, z], feature_peer(k),
        )

    def f_copy(k):
        block = wg.at[(pair + 4 - k) % 4, rows]
        return remote(block, block, sem_f_s.at[k], sem_f_r.at[k], other_core)

    def m_copy(t, k):
        return remote(part.at[t, k], parts_in.at[t, k], sem_m_s.at[t, k], sem_m_r.at[t, k], feature_peer(k))

    for copy in kv:
        copy.start()
    for t in range(splits):

        @pl.loop(1, GROUP)
        def _(o):
            q_copy(t, o).start()

    for k in range(1, 4):
        for z in range(NZH):
            w_copy(k, z).start()

    for load in loads:
        load.wait()
    lvt[...] = lv[...].T
    for i in range(2):
        vt[c * 2 + i] = vbuf[c * 2 + i].T
    hot = lax.broadcasted_iota(jnp.int32, gate.shape, 0) == step[0]
    gcol[...] = jnp.sum(jnp.where(hot, gate[...], 0.0).T, axis=1, keepdims=True)
    for copy in kv:
        copy.wait_recv()
    for i in range(2):
        vt[(1 - c) * 2 + i] = vbuf[(1 - c) * 2 + i].T

    def listed(block, holder):
        frame, live = 0, 0
        for j in range(4):
            slot = slot_of[windows[block, j]]
            hit = jnp.logical_and(j < counts[block], slot // 2 == holder).astype(jnp.int32)
            frame = frame + hit * (slot % 2)
            live = live + hit
        return frame, live

    def scores(keys, q):
        return lax.dot_general(keys, q, (((1,), (1,)), ((), ())), preferred_element_type=F32)

    def attend(t, o, own):
        q = qall[o, span(t)]
        dz, dx = o // NX, o % NX
        block = ((zl + dz) % NZL) * 8 + ((x - dx + NX) % NX) * 2 + c
        pieces = []
        tops = []
        for d in range(2):
            frame, live = listed(block, zl * 8 + x * 2 + d)
            s = scores(kbuf[2 * d + frame], q) * SCALE2
            on = jnp.full((1, width), live, jnp.int32) > 0
            tops.append(jnp.where(on, jnp.max(s, axis=0, keepdims=True), NEG))
            pieces.append((s, on, vt[2 * d + frame]))
        if own:
            s = scores(lk[...], q) * SCALE2
            tops.append(jnp.max(s, axis=0, keepdims=True))
            pieces.append((s, None, lvt[...]))
        m = functools.reduce(jnp.maximum, tops).astype(BF).astype(F32)
        total, result = 0.0, 0.0
        for s, on, values in pieces:
            shift = -m if on is None else jnp.where(on, -m, NEG)
            p = jnp.exp2(s + shift)
            total = total + jnp.sum(p, axis=0, keepdims=True)
            result = result + jnp.dot(values, p.astype(BF), preferred_element_type=F32)
        return m, total, result

    def attend_own(t):
        m, total, result = attend(t, 0, True)
        acc[t] = result
        top[t] = jnp.broadcast_to(m, (8, width))
        den[t] = jnp.broadcast_to(total, (8, width))

    def visit(t, first, last):

        @pl.loop(first, last)
        def _(o):
            q_copy(t, o).wait_recv()
            m, total, result = attend(t, o, False)
            sent[t, o, 0:HEAD] = result.astype(BF)
            high = total.astype(BF).astype(F32)
            row = lax.broadcasted_iota(jnp.int32, (16, width), 0)
            stats = jnp.where(row == 0, m, jnp.where(row == 1, high, total - high))
            sent[t, o, HEAD:MSG] = stats.astype(BF)
            p_copy(t, o).start()

    def merge(t):

        @pl.loop(1, GROUP)
        def _(o):
            p_copy(t, o).wait_recv()
            stats = came[t, o, HEAD:MSG].astype(F32)
            m = stats[0:1]
            total = stats[1:2] + stats[2:3]
            old = top[t, 0:1]
            new = jnp.maximum(old, m)
            keep = jnp.exp2(old - new)
            take = jnp.exp2(m - new)
            acc[t] = acc[t] * keep + came[t, o, 0:HEAD].astype(F32) * take
            den[t] = jnp.broadcast_to(den[t, 0:1] * keep + total * take, (8, width))
            top[t] = jnp.broadcast_to(new, (8, width))

        att[t, 2 * zh + side] = (acc[t] / den[t, 0:1]).astype(BF)

        @pl.loop(1, 8)
        def _(k):
            a_copy(t, k).start()

    def project(t):

        @pl.loop(1, 8)
        def _(k):
            a_copy(t, k).wait_recv()

        rows_in = att[t].reshape(COLS, width)

        @pl.loop(1, 4)
        def _(k):
            mixed = jnp.dot(wg[(pair + k) % 4], rows_in, preferred_element_type=F32)
            part[t, k] = mixed.astype(BF)
            m_copy(t, k).start()

        return jnp.dot(wg[pair], rows_in, preferred_element_type=F32)

    def finish(t, mixed):
        for k in range(1, 4):
            m_copy(t, k).wait_recv()
            mixed = mixed + parts_in[t, k].astype(F32)
        out_ref[:, span(t)] = (resid[:, span(t)].astype(F32) + gcol[...] * mixed).astype(BF)

    attend_own(0)
    visit(0, 1, GROUP)
    for t in range(1, splits):
        attend_own(t)
        visit(t, 1, GROUP // 2)
        merge(t - 1)
        visit(t, GROUP // 2, GROUP)
    merge(splits - 1)
    for k in range(1, 4):
        for z in range(NZH):
            w_copy(k, z).wait_recv()
        f_copy(k).start()
    for k in range(1, 4):
        f_copy(k).wait_recv()
    own_parts = [project(t) for t in range(splits)]
    for t in range(splits):
        finish(t, own_parts[t])

    for copy in kv:
        copy.wait_send()
    for t in range(splits):

        @pl.loop(1, GROUP)
        def _(o):
            q_copy(t, o).wait_send()
            p_copy(t, o).wait_send()

        @pl.loop(1, 8)
        def _(k):
            a_copy(t, k).wait_send()

        for k in range(1, 4):
            m_copy(t, k).wait_send()
    for k in range(1, 4):
        for z in range(NZH):
            w_copy(k, z).wait_send()
        f_copy(k).wait_send()


def local(splits, *args):
    width = TOK // splits
    anywhere = pl.BlockSpec(memory_space=pl.ANY)
    smem = pl.BlockSpec(memory_space=pltpu.SMEM)
    dma = pltpu.SemaphoreType.DMA
    return pl.pallas_call(
        functools.partial(kernel, splits),
        out_shape=jax.ShapeDtypeStruct((FEAT, TOK), BF),
        in_specs=[anywhere] * 5 + [smem] * 3 + [anywhere] * 3 + [smem],
        out_specs=pl.BlockSpec(memory_space=pltpu.VMEM),
        scratch_shapes=[
            pltpu.VMEM((GROUP, TOK, HEAD), BF),
            pltpu.VMEM((4, FRAME, HEAD), BF),
            pltpu.VMEM((4, FRAME, HEAD), BF),
            pltpu.VMEM((4, HEAD, FRAME), BF),
            pltpu.VMEM((TOK, HEAD), BF),
            pltpu.VMEM((TOK, HEAD), BF),
            pltpu.VMEM((HEAD, TOK), BF),
            pltpu.VMEM((splits, GROUP, MSG, width), BF),
            pltpu.VMEM((splits, GROUP, MSG, width), BF),
            pltpu.VMEM((splits, HEAD, width), F32),
            pltpu.VMEM((splits, 8, width), F32),
            pltpu.VMEM((splits, 8, width), F32),
            pltpu.VMEM((splits, 8, HEAD, width), BF),
            pltpu.VMEM((NZH, FEAT, COLS), BF),
            pltpu.VMEM((splits, NZH, FEAT, width), BF),
            pltpu.VMEM((splits, NZH, FEAT, width), BF),
            pltpu.VMEM((FEAT, TOK), BF),
            pltpu.VMEM((50, FEAT), F32),
            pltpu.VMEM((FEAT, 1), F32),
            dma((11,)),
            dma((2,)), dma((2,)),
            dma((splits, GROUP)), dma((splits, GROUP)),
            dma((splits, GROUP)), dma((splits, GROUP)),
            dma((splits, NY)), dma((splits, NY)),
            dma((4, NZH)), dma((4, NZH)),
            dma((4,)), dma((4,)),
            dma((splits, NZH)), dma((splits, NZH)),
        ],
        compiler_params=pltpu.CompilerParams(
            collective_id=0, has_side_effects=True, vmem_limit_bytes=60 << 20
        ),
        name="block_attention_projection",
    )(*args)


def solution(mesh):
    return jax.shard_map(
        functools.partial(local, 1),
        mesh=mesh,
        in_specs=(
            P("frames", "heads"),
            P("frames", "heads"),
            P("frames", "heads"),
            P("frames", None, "heads"),
            P("frames", None, "heads"),
            P(),
            P(),
            P(),
            P("heads", "frames"),
            P("heads", None),
            P(None, "heads"),
            P(),
        ),
        out_specs=P("heads", "frames"),
        check_vma=False,
    )
```

```python
import functools

import jax
import jax.numpy as jnp
from jax import lax
from jax.experimental import pallas as pl
from jax.experimental.pallas import tpu as pltpu
from jax.sharding import PartitionSpec as P

MESH = pl.DeviceIdType.MESH
BF = jnp.bfloat16
F32 = jnp.float32
NX, NZL, NC, NZH, NY = 4, 2, 2, 4, 8
GROUP = NX * NZL
HEAD = 128
TOK = 256
FRAME = 512
FEAT = 160
HALF_FEAT = FEAT // 2
COLS = 8 * HEAD
MSG = HEAD + 16
NEG = -(2.0**100)
SCALE2 = HEAD ** (-0.5) * 1.4426950408889634


def coords():
    f = lax.axis_index("frames")
    h = lax.axis_index("heads")
    return f // 8, (f // 2) % 4, f % 2, h // 8, h % 8


def device(zl, x, c, zh, y):
    return (zl * 8 + x * 2 + c, zh * 8 + y)


def kernel(
    splits,
    q_hbm, lk_hbm, lv_hbm, ck_hbm, cv_hbm, windows_hbm, counts_hbm, slots_hbm, res_hbm, w_hbm, gate_hbm, step_hbm,
    out_ref,
    qall, kbuf, vbuf, vt, lk, lv, lvt, sent, came, att, wg, part, parts_in, resid, gate, gcol,
    windows, counts, slot_of, step,
    sem_load, sem_kv_s, sem_kv_r, sem_q_s, sem_q_r, sem_p_s, sem_p_r,
    sem_a_s, sem_a_r, sem_w_s, sem_w_r, sem_f_s, sem_f_r, sem_m_s, sem_m_r,
):
    zl, x, c, zh, y = coords()
    width = TOK // splits
    pair, side = y // 2, y % 2

    def frame_peer(o, sign):
        dz, dx = o // NX, o % NX
        return device((zl + dz) % NZL, (x + sign * dx + NX) % NX, c, zh, y)

    def z_peer(k):
        return device(zl, x, c, (zh + k) % NZH, y)

    def feature_peer(k):
        return device(zl, x, c, zh, (y + 2 * k) % NY)

    other_core = device(zl, x, 1 - c, zh, y)
    other_side = device(zl, x, c, zh, 2 * pair + 1 - side)

    mine = pl.ds(pl.multiple_of(c * 2, 2), 2)
    near = [
        (ck_hbm, kbuf.at[mine]), (cv_hbm, vbuf.at[mine]), (q_hbm, qall.at[0]), (lk_hbm, lk), (lv_hbm, lv),
        (windows_hbm, windows), (counts_hbm, counts), (slots_hbm, slot_of), (step_hbm, step), (gate_hbm, gate),
        (res_hbm, resid),
    ]
    for z in range(NZH):
        near.append((
            w_hbm.at[:, pl.ds(pl.multiple_of(z * 1024 + pair * 256, 256), 256)],
            wg.at[pair, :, pl.ds(z * 256, 256)],
        ))
    loads = [pltpu.make_async_copy(src, dst, sem_load.at[i]) for i, (src, dst) in enumerate(near)]
    for load in loads:
        load.start()

    barrier = pltpu.get_barrier_semaphore()
    peers = [other_core, other_side]
    peers += [frame_peer(o, 1) for o in range(1, GROUP)]
    peers += [z_peer(k) for k in range(1, NZH)]
    peers += [feature_peer(k) for k in range(1, 4)]
    for peer in peers:
        pl.semaphore_signal(barrier, inc=1, device_id=peer, device_id_type=MESH)
    pl.semaphore_wait(barrier, len(peers))

    def remote(src, dst, send, recv, peer):
        return pltpu.make_async_remote_copy(
            src_ref=src, dst_ref=dst, send_sem=send, recv_sem=recv, device_id=peer, device_id_type=MESH
        )

    def span(t):
        return pl.ds(t * width, width)

    kv = [
        remote(ck_hbm, kbuf.at[mine], sem_kv_s.at[0], sem_kv_r.at[0], other_core),
        remote(cv_hbm, vbuf.at[mine], sem_kv_s.at[1], sem_kv_r.at[1], other_core),
    ]

    def q_copy(t, o):
        return remote(
            q_hbm.at[span(t)], qall.at[o, span(t)], sem_q_s.at[t, o], sem_q_r.at[t, o], frame_peer(o, 1)
        )

    def p_copy(t, o):
        return remote(sent.at[t, o], came.at[t, o], sem_p_s.at[t, o], sem_p_r.at[t, o], frame_peer(o, -1))

    def a_copy(t, k):
        here = att.at[t, 2 * ((zh + (0 if k < 4 else 8 - k)) % NZH) + side]
        peer = z_peer(k) if 0 < k < 4 else other_side
        return remote(here, here, sem_a_s.at[t, k], sem_a_r.at[t, k], peer)

    rows = pl.ds(pl.multiple_of(c * HALF_FEAT, 16), HALF_FEAT)

    def w_copy(k, z):
        there = (pair + k) % 4
        return remote(
            w_hbm.at[rows, pl.ds(pl.multiple_of(z * 1024 + there * 256, 256), 256)],
            wg.at[pair, rows, pl.ds(z * 256, 256)], sem_w_s.at[k, z], sem_w_r.at[k, z], feature_peer(k),
        )

    def f_copy(k):
        block = wg.at[(pair + 4 - k) % 4, rows]
        return remote(block, block, sem_f_s.at[k], sem_f_r.at[k], other_core)

    def m_copy(t, k):
        return remote(part.at[t, k], parts_in.at[t, k], sem_m_s.at[t, k], sem_m_r.at[t, k], feature_peer(k))

    q_order = [1, 4, 3, 2, 5, 7, 6]
    for copy in kv:
        copy.start()
    for t in range(splits):
        for o in q_order:
            q_copy(t, o).start()
    if W_ON:
        for k in (2, 1, 3):
            for z in range(NZH):
                w_copy(k, z).start()

    for load in loads:
        load.wait()
    lvt[...] = lv[...].T
    for i in range(2):
        vt[c * 2 + i] = vbuf[c * 2 + i].T
    hot = lax.broadcasted_iota(jnp.int32, gate.shape, 0) == step[0]
    gcol[...] = jnp.sum(jnp.where(hot, gate[...], 0.0).T, axis=1, keepdims=True)
    for copy in kv:
        copy.wait_recv()
    for i in range(2):
        vt[(1 - c) * 2 + i] = vbuf[(1 - c) * 2 + i].T

    def listed(block, holder):
        frame, live = 0, 0
        for j in range(4):
            slot = slot_of[windows[j, block]]
            hit = jnp.logical_and(j < counts[block], slot // 2 == holder).astype(jnp.int32)
            frame = frame + hit * (slot % 2)
            live = live + hit
        return frame, live

    def scores(keys, q):
        return lax.dot_general(keys, q, (((1,), (1,)), ((), ())), preferred_element_type=F32)

    def attend(t, offsets):
        units = []
        for o in offsets:
            q = qall[o, span(t)]
            dz, dx = o // NX, o % NX
            block = ((zl + dz) % NZL) * 8 + ((x - dx + NX) % NX) * 2 + c
            pieces = []
            for d in range(2):
                frame, live = listed(block, zl * 8 + x * 2 + d)
                pieces.append((scores(kbuf[2 * d + frame], q), jnp.full((1, width), live, jnp.int32) > 0, vt.at[2 * d + frame]))
            if o == 0:
                pieces.append((scores(lk[...], q), None, lvt))
            units.append(pieces)
        results = []
        for pieces in units:
            tops = []
            for s, on, _ in pieces:
                top = jnp.max(s, axis=0, keepdims=True) * SCALE2
                tops.append(top if on is None else jnp.where(on, top, NEG))
            m = functools.reduce(jnp.maximum, tops).astype(BF).astype(F32)
            total, result = 0.0, 0.0
            for s, on, values in pieces:
                p = jnp.exp2(s * SCALE2 + (-m if on is None else jnp.where(on, -m, NEG)))
                total = total + jnp.sum(p, axis=0, keepdims=True)
                result = result + jnp.dot(values[...], p.astype(BF), preferred_element_type=F32)
            results.append((m, total, result))
        return results

    def visit(t, offsets):
        for o in offsets:
            if o > 0:
                q_copy(t, o).wait_recv()
        for o, (m, total, result) in zip(offsets, attend(t, offsets)):
            high = total.astype(BF).astype(F32)
            row = lax.broadcasted_iota(jnp.int32, (16, width), 0)
            stats = jnp.where(row == 0, m, jnp.where(row == 1, high, total - high))
            sent[t, o, 0:HEAD] = result.astype(BF)
            sent[t, o, HEAD:MSG] = stats.astype(BF)
            if o > 0:
                p_copy(t, o).start()

    def merge(t):
        for o in range(1, GROUP):
            p_copy(t, o).wait_recv()
        stats = [(sent if o == 0 else came)[t, o, HEAD:MSG].astype(F32) for o in range(GROUP)]
        m = functools.reduce(jnp.maximum, [each[0:1] for each in stats])
        total, result = 0.0, 0.0
        for o in range(GROUP):
            share = jnp.exp2(stats[o][0:1] - m)
            total = total + share * (stats[o][1:2] + stats[o][2:3])
            result = result + share * (sent if o == 0 else came)[t, o, 0:HEAD].astype(F32)
        att[t, 2 * zh + side] = (result / total).astype(BF)
        for k in (2, 1, 3, 0):
            a_copy(t, k).start()

    def spread(t):
        for k in (1, 3, 2):
            a_copy(t, k).wait_recv()
            a_copy(t, 4 + k).start()

    def project(t):
        for k in (0, 5, 7, 6):
            a_copy(t, k).wait_recv()
        rows_in = att[t].reshape(COLS, width)
        for k in (2, 1, 3):
            mixed = jnp.dot(wg[(pair + k) % 4], rows_in, preferred_element_type=F32)
            part[t, k] = mixed.astype(BF)
            m_copy(t, k).start()
        return jnp.dot(wg[pair], rows_in, preferred_element_type=F32)

    def finish(t, mixed):
        for k in (1, 3, 2):
            m_copy(t, k).wait_recv()
            mixed = mixed + parts_in[t, k].astype(F32)
        out_ref[:, span(t)] = (resid[:, span(t)].astype(F32) + gcol[...] * mixed).astype(BF)

    def forward_weights():
        for k in (1, 3, 2):
            for z in range(NZH):
                w_copy(k, z).wait_recv()
            f_copy(k).start()

    first, second = [0, 1, 4, 3], [2, 5, 7, 6]
    visit(0, first)
    visit(0, second)
    if splits == 2:
        visit(1, first)
        merge(0)
        visit(1, second)
        spread(0)
    merge(splits - 1)
    if W_ON:
        forward_weights()
    spread(splits - 1)
    if W_ON:
        for k in (1, 3, 2):
            f_copy(k).wait_recv()
    own_parts = [project(t) for t in range(splits)]
    for t in range(splits):
        finish(t, own_parts[t])

    for copy in kv:
        copy.wait_send()
    for t in range(splits):
        for o in range(1, GROUP):
            q_copy(t, o).wait_send()
            p_copy(t, o).wait_send()
        for k in (0, 1, 2, 3, 5, 6, 7):
            a_copy(t, k).wait_send()
        for k in range(1, 4):
            m_copy(t, k).wait_send()
    if W_ON:
        for k in range(1, 4):
            for z in range(NZH):
                w_copy(k, z).wait_send()
            f_copy(k).wait_send()


W_ON = True


def local(splits, q, lk, lv, ck, cv, windows, *args):
    width = TOK // splits
    hbm = pl.BlockSpec(memory_space=pltpu.HBM)
    dma = pltpu.SemaphoreType.DMA
    return pl.pallas_call(
        functools.partial(kernel, splits),
        out_shape=jax.ShapeDtypeStruct((FEAT, TOK), BF),
        in_specs=[hbm] * 12,
        out_specs=pl.BlockSpec(memory_space=pltpu.VMEM),
        scratch_shapes=[
            pltpu.VMEM((GROUP, TOK, HEAD), BF),
            pltpu.VMEM((4, FRAME, HEAD), BF),
            pltpu.VMEM((4, FRAME, HEAD), BF),
            pltpu.VMEM((4, HEAD, FRAME), BF),
            pltpu.VMEM((TOK, HEAD), BF),
            pltpu.VMEM((TOK, HEAD), BF),
            pltpu.VMEM((HEAD, TOK), BF),
            pltpu.VMEM((splits, GROUP, MSG, width), BF),
            pltpu.VMEM((splits, GROUP, MSG, width), BF),
            pltpu.VMEM((splits, 8, HEAD, width), BF),
            pltpu.VMEM((4, FEAT, COLS), BF),
            pltpu.VMEM((splits, 4, FEAT, width), BF),
            pltpu.VMEM((splits, 4, FEAT, width), BF),
            pltpu.VMEM((FEAT, TOK), BF),
            pltpu.VMEM((50, FEAT), F32),
            pltpu.VMEM((FEAT, 1), F32),
            pltpu.SMEM((4, 16), jnp.int32),
            pltpu.SMEM((16,), jnp.int32),
            pltpu.SMEM((32,), jnp.int32),
            pltpu.SMEM((1,), jnp.int32),
            dma((15,)),
            dma((2,)), dma((2,)),
            dma((splits, GROUP)), dma((splits, GROUP)),
            dma((splits, GROUP)), dma((splits, GROUP)),
            dma((splits, 8)), dma((splits, 8)),
            dma((4, NZH)), dma((4, NZH)),
            dma((4,)), dma((4,)),
            dma((splits, 4)), dma((splits, 4)),
        ],
        compiler_params=pltpu.CompilerParams(
            collective_id=0, has_side_effects=True, vmem_limit_bytes=60 << 20
        ),
        name="block_attention_projection",
    )(q, lk, lv, ck, cv, windows.T, *args)


def solution(mesh):
    return jax.shard_map(
        functools.partial(local, 2),
        mesh=mesh,
        in_specs=(
            P("frames", "heads"),
            P("frames", "heads"),
            P("frames", "heads"),
            P("frames", None, "heads"),
            P("frames", None, "heads"),
            P(),
            P(),
            P(),
            P("heads", "frames"),
            P("heads", None),
            P(None, "heads"),
            P(),
        ),
        out_specs=P("heads", "frames"),
        check_vma=False,
    )
```

```python
import functools

import jax
import jax.numpy as jnp
from jax import lax
from jax.experimental import pallas as pl
from jax.experimental.pallas import tpu as pltpu
from jax.sharding import PartitionSpec as P

MESH = pl.DeviceIdType.MESH
BF = jnp.bfloat16
F32 = jnp.float32
NX, NZL, NC, NZH, NY = 4, 2, 2, 4, 8
GROUP = NX * NZL
HEAD = 128
TOK = 256
FRAME = 512
FEAT = 160
COLS = 8 * HEAD
MSG = HEAD + 16
NEG = -(2.0**100)
SCALE2 = HEAD ** (-0.5) * 1.4426950408889634


def coords():
    f = lax.axis_index("frames")
    h = lax.axis_index("heads")
    return f // 8, (f // 2) % 4, f % 2, h // 8, h % 8


def device(zl, x, c, zh, y):
    return (zl * 8 + x * 2 + c, zh * 8 + y)


def kernel(
    splits,
    q_hbm, lk_hbm, lv_hbm, ck_hbm, cv_hbm, windows_hbm, counts_hbm, slots_hbm, res_hbm, w_hbm, gate_hbm, step_hbm,
    out_ref,
    qall, kbuf, vbuf, vt, lk, lv, lvt, sent, came, att, wg, part, parts_in, resid, gate, gcol,
    windows, counts, slot_of, step,
    sem_load, sem_kv_s, sem_kv_r, sem_q_s, sem_q_r, sem_p_s, sem_p_r,
    sem_a_s, sem_a_r, sem_w_s, sem_w_r, sem_m_s, sem_m_r,
):
    zl, x, c, zh, y = coords()
    width = TOK // splits
    even = 1 - c
    pair, side = y // 2, y % 2
    my_set = even * pair + c * zh
    my_slot = even * (2 * zh + side) + c * y

    def frame_peer(o, sign):
        dz, dx = o // NX, o % NX
        return device((zl + dz) % NZL, (x + sign * dx + NX) % NX, c, zh, y)

    def set_peer(k):
        slot = (my_slot + k) % 8
        return device(zl, x, c, even * (slot // 2) + c * zh, even * (2 * pair + slot % 2) + c * slot)

    def feature_peer(k):
        there = (my_set + k) % 4
        return device(zl, x, c, even * zh + c * there, even * (2 * there + side) + c * y)

    def columns(there, i):
        start = (even * i + c * there) * 1024 + (even * there + c * i) * 256
        return pl.ds(pl.multiple_of(start, 256), 256)

    other_core = device(zl, x, 1 - c, zh, y)

    mine = pl.ds(pl.multiple_of(c * 2, 2), 2)
    near = [
        (ck_hbm, kbuf.at[mine]), (cv_hbm, vbuf.at[mine]), (q_hbm, qall.at[0]), (lk_hbm, lk), (lv_hbm, lv),
        (windows_hbm, windows), (counts_hbm, counts), (slots_hbm, slot_of), (step_hbm, step), (gate_hbm, gate),
        (res_hbm, resid),
    ]
    for i in range(4):
        near.append((w_hbm.at[:, columns(my_set, i)], wg.at[my_set, :, pl.ds(i * 256, 256)]))
    loads = [pltpu.make_async_copy(src, dst, sem_load.at[i]) for i, (src, dst) in enumerate(near)]
    barrier = pltpu.get_barrier_semaphore()
    peers = [frame_peer(o, 1) for o in range(1, GROUP)]
    peers += [other_core]
    peers += [set_peer(k) for k in range(1, 8)]
    peers += [feature_peer(k) for k in range(1, 4)]
    for peer in peers:
        pl.semaphore_signal(barrier, inc=1, device_id=peer, device_id_type=MESH)
    for load in loads:
        load.start()
    pl.semaphore_wait(barrier, len(peers))

    def remote(src, dst, send, recv, peer):
        return pltpu.make_async_remote_copy(
            src_ref=src, dst_ref=dst, send_sem=send, recv_sem=recv, device_id=peer, device_id_type=MESH
        )

    def span(t):
        return pl.ds(t * width, width)

    kv = [
        remote(ck_hbm, kbuf.at[mine], sem_kv_s.at[0], sem_kv_r.at[0], other_core),
        remote(cv_hbm, vbuf.at[mine], sem_kv_s.at[1], sem_kv_r.at[1], other_core),
    ]

    def q_copy(t, o):
        return remote(
            q_hbm.at[span(t)], qall.at[o, span(t)], sem_q_s.at[t, o], sem_q_r.at[t, o], frame_peer(o, 1)
        )

    def p_copy(t, o):
        return remote(sent.at[t, o], came.at[t, o], sem_p_s.at[t, o], sem_p_r.at[t, o], frame_peer(o, -1))

    def a_copy(t, k):
        here = att.at[t, my_slot]
        return remote(here, here, sem_a_s.at[t, k], sem_a_r.at[t, k], set_peer(k))

    def w_copy(k, i):
        return remote(
            w_hbm.at[:, columns((my_set + k) % 4, i)],
            wg.at[my_set, :, pl.ds(i * 256, 256)], sem_w_s.at[k, i], sem_w_r.at[k, i], feature_peer(k),
        )

    def quarter_copy(k):
        return remote(
            w_hbm.at[:, columns((my_set + k) % 4, x)],
            wg.at[my_set, :, pl.ds(pl.multiple_of(x * 256, 256), 256)],
            sem_w_s.at[k, 0], sem_w_r.at[k, 0], feature_peer(k),
        )

    def x_copy(k, d):
        block = wg.at[(my_set + 4 - k) % 4, :, pl.ds(pl.multiple_of(x * 256, 256), 256)]
        return remote(block, block, sem_w_s.at[k, d], sem_w_r.at[k, d], frame_peer(d, 1))

    def m_copy(t, k):
        return remote(part.at[t, k], parts_in.at[t, k], sem_m_s.at[t, k], sem_m_r.at[t, k], feature_peer(k))

    for copy in kv:
        copy.start()
    first, second = [0, 1, 4, 3], [5, 7, 2, 6]
    orders = (first + second, second[::-1] + first)
    for t in range(splits):
        for o in orders[t]:
            if o > 0:
                q_copy(t, o).start()
    for load in loads:
        load.wait()

    quarter_copy(2).start()

    @pl.when(c == 0)
    def _():
        for k in (1, 3):
            for i in range(4):
                w_copy(k, i).start()

    @pl.when(c == 1)
    def _():
        for k in (1, 3):
            quarter_copy(k).start()

    lvt[...] = lv[...].T
    for i in range(2):
        vt[c * 2 + i] = vbuf[c * 2 + i].T
    hot = lax.broadcasted_iota(jnp.int32, gate.shape, 0) == step[0]
    gcol[...] = jnp.sum(jnp.where(hot, gate[...], 0.0).T, axis=1, keepdims=True)
    for copy in kv:
        copy.wait_recv()
    for i in range(2):
        vt[(1 - c) * 2 + i] = vbuf[(1 - c) * 2 + i].T

    def listed(block, holder):
        frame, live = 0, 0
        for j in range(4):
            slot = slot_of[windows[j, block]]
            hit = jnp.logical_and(j < counts[block], slot // 2 == holder).astype(jnp.int32)
            frame = frame + hit * (slot % 2)
            live = live + hit
        return frame, live

    def scores(keys, q):
        return lax.dot_general(keys, q, (((1,), (1,)), ((), ())), preferred_element_type=F32)

    def attend(t, offsets):
        units = []
        for o in offsets:
            q = qall[o, span(t)]
            dz, dx = o // NX, o % NX
            block = ((zl + dz) % NZL) * 8 + ((x - dx + NX) % NX) * 2 + c
            pieces = []
            for d in range(2):
                frame, live = listed(block, zl * 8 + x * 2 + d)
                pieces.append((scores(kbuf[2 * d + frame], q), jnp.full((1, width), live, jnp.int32) > 0, vt.at[2 * d + frame]))
            if o == 0:
                pieces.append((scores(lk[...], q), None, lvt))
            units.append(pieces)
        results = []
        for pieces in units:
            tops = []
            for s, on, _ in pieces:
                top = jnp.max(s, axis=0, keepdims=True) * SCALE2
                tops.append(top if on is None else jnp.where(on, top, NEG))
            m = functools.reduce(jnp.maximum, tops).astype(BF).astype(F32)
            total, result = 0.0, 0.0
            for s, on, values in pieces:
                p = jnp.exp2(s * SCALE2 + (-m if on is None else jnp.where(on, -m, NEG)))
                total = total + jnp.sum(p, axis=0, keepdims=True)
                result = result + jnp.dot(values[...], p.astype(BF), preferred_element_type=F32)
            results.append((m, total, result))
        return results

    def visit(t, offsets):
        for o in offsets:
            if o > 0:
                q_copy(t, o).wait_recv()
        for o, (m, total, result) in zip(offsets, attend(t, offsets)):
            high = total.astype(BF).astype(F32)
            row = lax.broadcasted_iota(jnp.int32, (16, width), 0)
            stats = jnp.where(row == 0, m, jnp.where(row == 1, high, total - high))
            sent[t, o, 0:HEAD] = result.astype(BF)
            sent[t, o, HEAD:MSG] = stats.astype(BF)
            if o > 0:
                p_copy(t, o).start()

    def merge(t):
        for o in range(1, GROUP):
            p_copy(t, o).wait_recv()
        stats = [(sent if o == 0 else came)[t, o, HEAD:MSG].astype(F32) for o in range(GROUP)]
        m = functools.reduce(jnp.maximum, [each[0:1] for each in stats])
        total, result = 0.0, 0.0
        for o in range(GROUP):
            share = jnp.exp2(stats[o][0:1] - m)
            total = total + share * (stats[o][1:2] + stats[o][2:3])
            result = result + share * (sent if o == 0 else came)[t, o, 0:HEAD].astype(F32)
        att[t, my_slot] = (result / total).astype(BF)
        for k in (4, 3, 5, 2, 6, 1, 7):
            a_copy(t, k).start()

    def project(t):
        for k in range(1, 8):
            a_copy(t, k).wait_recv()
        rows_in = att[t].reshape(COLS, width)
        for k in (2, 1, 3):
            mixed = jnp.dot(wg[(my_set + k) % 4], rows_in, preferred_element_type=F32)
            part[t, k] = mixed.astype(BF)
            m_copy(t, k).start()
        return jnp.dot(wg[my_set], rows_in, preferred_element_type=F32)

    def finish(t, mixed):
        for k in (1, 3, 2):
            m_copy(t, k).wait_recv()
            mixed = mixed + parts_in[t, k].astype(F32)
        out_ref[:, span(t)] = (resid[:, span(t)].astype(F32) + gcol[...] * mixed).astype(BF)

    def share_weights():

        def share(k):
            quarter_copy(k).wait_recv()
            for d in (2, 1, 3):
                x_copy(k, d).start()

        share(2)

        @pl.when(c == 1)
        def _():
            share(1)
            share(3)

    def await_weights():

        @pl.when(c == 0)
        def _():
            for k in (1, 3):
                for i in range(4):
                    w_copy(k, i).wait_recv()

        @pl.when(c == 1)
        def _():
            for k in (1, 3):
                for d in (1, 3, 2):
                    x_copy(k, d).wait_recv()

        for d in (1, 3, 2):
            x_copy(2, d).wait_recv()

    visit(0, first)
    visit(0, second)
    visit(1, second[::-1])
    visit(1, first)
    merge(0)
    share_weights()
    merge(1)
    await_weights()
    own_parts = [project(t) for t in range(splits)]
    for t in range(splits):
        finish(t, own_parts[t])

    for copy in kv:
        copy.wait_send()
    for t in range(splits):
        for o in range(1, GROUP):
            q_copy(t, o).wait_send()
            p_copy(t, o).wait_send()
        for k in range(1, 8):
            a_copy(t, k).wait_send()
        for k in range(1, 4):
            m_copy(t, k).wait_send()
    def drain(k):
        quarter_copy(k).wait_send()
        for d in range(1, 4):
            x_copy(k, d).wait_send()

    drain(2)

    @pl.when(c == 0)
    def _():
        for k in (1, 3):
            for i in range(4):
                w_copy(k, i).wait_send()

    @pl.when(c == 1)
    def _():
        drain(1)
        drain(3)


def local(splits, q, lk, lv, ck, cv, windows, *args):
    width = TOK // splits
    hbm = pl.BlockSpec(memory_space=pltpu.HBM)
    dma = pltpu.SemaphoreType.DMA
    return pl.pallas_call(
        functools.partial(kernel, splits),
        out_shape=jax.ShapeDtypeStruct((FEAT, TOK), BF),
        in_specs=[hbm] * 12,
        out_specs=pl.BlockSpec(memory_space=pltpu.VMEM),
        scratch_shapes=[
            pltpu.VMEM((GROUP, TOK, HEAD), BF),
            pltpu.VMEM((4, FRAME, HEAD), BF),
            pltpu.VMEM((4, FRAME, HEAD), BF),
            pltpu.VMEM((4, HEAD, FRAME), BF),
            pltpu.VMEM((TOK, HEAD), BF),
            pltpu.VMEM((TOK, HEAD), BF),
            pltpu.VMEM((HEAD, TOK), BF),
            pltpu.VMEM((splits, GROUP, MSG, width), BF),
            pltpu.VMEM((splits, GROUP, MSG, width), BF),
            pltpu.VMEM((splits, 8, HEAD, width), BF),
            pltpu.VMEM((4, FEAT, COLS), BF),
            pltpu.VMEM((splits, 4, FEAT, width), BF),
            pltpu.VMEM((splits, 4, FEAT, width), BF),
            pltpu.VMEM((FEAT, TOK), BF),
            pltpu.VMEM((50, FEAT), F32),
            pltpu.VMEM((FEAT, 1), F32),
            pltpu.SMEM((4, 16), jnp.int32),
            pltpu.SMEM((16,), jnp.int32),
            pltpu.SMEM((32,), jnp.int32),
            pltpu.SMEM((1,), jnp.int32),
            dma((15,)),
            dma((2,)), dma((2,)),
            dma((splits, GROUP)), dma((splits, GROUP)),
            dma((splits, GROUP)), dma((splits, GROUP)),
            dma((splits, 8)), dma((splits, 8)),
            dma((4, NZH)), dma((4, NZH)),
            dma((splits, 4)), dma((splits, 4)),
        ],
        compiler_params=pltpu.CompilerParams(
            collective_id=0, has_side_effects=True, vmem_limit_bytes=60 << 20
        ),
        name="block_attention_projection",
    )(q, lk, lv, ck, cv, windows.T, *args)


def solution(mesh):
    return jax.shard_map(
        functools.partial(local, 2),
        mesh=mesh,
        in_specs=(
            P("frames", "heads"),
            P("frames", "heads"),
            P("frames", "heads"),
            P("frames", None, "heads"),
            P("frames", None, "heads"),
            P(),
            P(),
            P(),
            P("heads", "frames"),
            P("heads", None),
            P(None, "heads"),
            P(),
        ),
        out_specs=P("heads", "frames"),
        check_vma=False,
    )
```

```python
import functools

import jax
import jax.numpy as jnp
from jax import lax
from jax.experimental import pallas as pl
from jax.experimental.pallas import tpu as pltpu
from jax.sharding import PartitionSpec as P

MESH = pl.DeviceIdType.MESH
BF = jnp.bfloat16
F32 = jnp.float32
NX, NZL, NC, NZH, NY = 4, 2, 2, 4, 8
GROUP = NX * NZL
HEAD = 128
TOK = 256
FRAME = 512
FEAT = 160
COLS = 8 * HEAD
MSG = HEAD + 16
NEG = -(2.0**100)
SCALE2 = HEAD ** (-0.5) * 1.4426950408889634


def coords():
    f = lax.axis_index("frames")
    h = lax.axis_index("heads")
    return f // 8, (f // 2) % 4, f % 2, h // 8, h % 8


def device(zl, x, c, zh, y):
    return (zl * 8 + x * 2 + c, zh * 8 + y)


def kernel(
    splits,
    q_hbm, lk_hbm, lv_hbm, ck_hbm, cv_hbm, windows_hbm, counts_hbm, slots_hbm, res_hbm, w_hbm, gate_hbm, step_hbm,
    out_ref,
    qall, kbuf, vbuf, vt, lk, lv, lvt, sent, came, att, wg, part, parts_in, resid, gate, gcol,
    windows, counts, slot_of, step,
    sem_load, sem_kv_s, sem_kv_r, sem_q_s, sem_q_r, sem_p_s, sem_p_r,
    sem_a_s, sem_a_r, sem_w_s, sem_w_r, sem_m_s, sem_m_r,
):
    zl, x, c, zh, y = coords()
    width = TOK // splits
    even = 1 - c
    pair, side = y // 2, y % 2
    my_set = even * pair + c * zh
    my_slot = even * (2 * zh + side) + c * y

    def frame_peer(o, sign):
        dz, dx = o // NX, o % NX
        return device((zl + dz) % NZL, (x + sign * dx + NX) % NX, c, zh, y)

    def set_peer(k):
        slot = (my_slot + k) % 8
        return device(zl, x, c, even * (slot // 2) + c * zh, even * (2 * pair + slot % 2) + c * slot)

    def feature_peer(k):
        there = (my_set + k) % 4
        return device(zl, x, c, even * zh + c * there, even * (2 * there + side) + c * y)

    def columns(there, i):
        start = (even * i + c * there) * 1024 + (even * there + c * i) * 256
        return pl.ds(pl.multiple_of(start, 256), 256)

    other_core = device(zl, x, 1 - c, zh, y)

    mine = pl.ds(pl.multiple_of(c * 2, 2), 2)
    near = [
        (ck_hbm, kbuf.at[mine]), (cv_hbm, vbuf.at[mine]), (q_hbm, qall.at[0]), (lk_hbm, lk), (lv_hbm, lv),
        (windows_hbm, windows), (counts_hbm, counts), (slots_hbm, slot_of), (step_hbm, step), (gate_hbm, gate),
        (res_hbm, resid),
    ]
    for i in range(4):
        near.append((w_hbm.at[:, columns(my_set, i)], wg.at[my_set, :, pl.ds(i * 256, 256)]))
    loads = [pltpu.make_async_copy(src, dst, sem_load.at[i]) for i, (src, dst) in enumerate(near)]
    barrier = pltpu.get_barrier_semaphore()
    peers = [frame_peer(o, 1) for o in range(1, GROUP)]
    peers += [other_core]
    peers += [set_peer(k) for k in range(1, 8)]
    peers += [feature_peer(k) for k in range(1, 4)]
    for peer in peers:
        pl.semaphore_signal(barrier, inc=1, device_id=peer, device_id_type=MESH)
    for load in loads:
        load.start()
    pl.semaphore_wait(barrier, len(peers))

    def remote(src, dst, send, recv, peer):
        return pltpu.make_async_remote_copy(
            src_ref=src, dst_ref=dst, send_sem=send, recv_sem=recv, device_id=peer, device_id_type=MESH
        )

    def span(t):
        return pl.ds(t * width, width)

    kv = [
        remote(ck_hbm, kbuf.at[mine], sem_kv_s.at[0], sem_kv_r.at[0], other_core),
        remote(cv_hbm, vbuf.at[mine], sem_kv_s.at[1], sem_kv_r.at[1], other_core),
    ]

    def q_copy(t, o):
        return remote(
            q_hbm.at[span(t)], qall.at[o, span(t)], sem_q_s.at[t, o], sem_q_r.at[t, o], frame_peer(o, 1)
        )

    def p_copy(t, o):
        return remote(sent.at[t, o], came.at[t, o], sem_p_s.at[t, o], sem_p_r.at[t, o], frame_peer(o, -1))

    def a_copy(t, k):
        here = att.at[t, my_slot]
        return remote(here, here, sem_a_s.at[t, k], sem_a_r.at[t, k], set_peer(k))

    def w_copy(k, i):
        return remote(
            w_hbm.at[:, columns((my_set + k) % 4, i)],
            wg.at[my_set, :, pl.ds(i * 256, 256)], sem_w_s.at[k, i], sem_w_r.at[k, i], feature_peer(k),
        )

    def quarter_copy(k):
        return remote(
            w_hbm.at[:, columns((my_set + k) % 4, x)],
            wg.at[my_set, :, pl.ds(pl.multiple_of(x * 256, 256), 256)],
            sem_w_s.at[k, 0], sem_w_r.at[k, 0], feature_peer(k),
        )

    def x_copy(k, d):
        block = wg.at[(my_set + 4 - k) % 4, :, pl.ds(pl.multiple_of(x * 256, 256), 256)]
        return remote(block, block, sem_w_s.at[k, d], sem_w_r.at[k, d], frame_peer(d, 1))

    def m_copy(t, k):
        return remote(part.at[t, k], parts_in.at[t, k], sem_m_s.at[t, k], sem_m_r.at[t, k], feature_peer(k))

    for copy in kv:
        copy.start()
    first, second = [0, 1, 4, 3], [5, 7, 2, 6]
    orders = (first + second, second[::-1] + first)
    for t in range(splits):
        for o in orders[t]:
            if o > 0:
                q_copy(t, o).start()
    for load in loads:
        load.wait()

    quarter_copy(2).start()

    @pl.when(c == 0)
    def _():
        for k in (1, 3):
            for i in range(4):
                w_copy(k, i).start()

    @pl.when(c == 1)
    def _():
        for k in (1, 3):
            quarter_copy(k).start()

    lvt[...] = lv[...].T
    for i in range(2):
        vt[c * 2 + i] = vbuf[c * 2 + i].T
    hot = lax.broadcasted_iota(jnp.int32, gate.shape, 0) == step[0]
    gcol[...] = jnp.sum(jnp.where(hot, gate[...], 0.0).T, axis=1, keepdims=True)
    for copy in kv:
        copy.wait_recv()
    for i in range(2):
        vt[(1 - c) * 2 + i] = vbuf[(1 - c) * 2 + i].T

    def listed(block, holder):
        frame, live = 0, 0
        for j in range(4):
            slot = slot_of[windows[j, block]]
            hit = jnp.logical_and(j < counts[block], slot // 2 == holder).astype(jnp.int32)
            frame = frame + hit * (slot % 2)
            live = live + hit
        return frame, live

    def scores(keys, q):
        return lax.dot_general(keys, q, (((1,), (1,)), ((), ())), preferred_element_type=F32)

    def attend(t, offsets):
        units = []
        for o in offsets:
            q = qall[o, span(t)]
            dz, dx = o // NX, o % NX
            block = ((zl + dz) % NZL) * 8 + ((x - dx + NX) % NX) * 2 + c
            pieces = []
            for d in range(2):
                frame, live = listed(block, zl * 8 + x * 2 + d)
                pieces.append((scores(kbuf[2 * d + frame], q), jnp.full((1, width), live, jnp.int32) > 0, vt.at[2 * d + frame]))
            if o == 0:
                pieces.append((scores(lk[...], q), None, lvt))
            units.append(pieces)
        results = []
        for pieces in units:
            tops = []
            for s, on, _ in pieces:
                top = jnp.max(s, axis=0, keepdims=True) * SCALE2
                tops.append(top if on is None else jnp.where(on, top, NEG))
            m = functools.reduce(jnp.maximum, tops).astype(BF).astype(F32)
            total, result = 0.0, 0.0
            for s, on, values in pieces:
                p = jnp.exp2(s * SCALE2 + (-m if on is None else jnp.where(on, -m, NEG)))
                total = total + jnp.sum(p, axis=0, keepdims=True)
                result = result + jnp.dot(values[...], p.astype(BF), preferred_element_type=F32)
            results.append((m, total, result))
        return results

    def visit(t, offsets):
        for o in offsets:
            if o > 0:
                q_copy(t, o).wait_recv()
        for o, (m, total, result) in zip(offsets, attend(t, offsets)):
            high = total.astype(BF).astype(F32)
            row = lax.broadcasted_iota(jnp.int32, (16, width), 0)
            stats = jnp.where(row == 0, m, jnp.where(row == 1, high, total - high))
            sent[t, o, 0:HEAD] = result.astype(BF)
            sent[t, o, HEAD:MSG] = stats.astype(BF)
            if o > 0:
                p_copy(t, o).start()

    def merge(t):
        for o in range(1, GROUP):
            p_copy(t, o).wait_recv()
        stats = [(sent if o == 0 else came)[t, o, HEAD:MSG].astype(F32) for o in range(GROUP)]
        m = functools.reduce(jnp.maximum, [each[0:1] for each in stats])
        total, result = 0.0, 0.0
        for o in range(GROUP):
            share = jnp.exp2(stats[o][0:1] - m)
            total = total + share * (stats[o][1:2] + stats[o][2:3])
            result = result + share * (sent if o == 0 else came)[t, o, 0:HEAD].astype(F32)
        att[t, my_slot] = (result / total).astype(BF)
        for slot in range(8):

            @pl.when(slot != my_slot)
            def _():
                a_copy(t, (slot - my_slot + 8) % 8).start()

    def project(t):
        for k in range(1, 8):
            a_copy(t, k).wait_recv()

        def product(there):
            return jnp.dot(wg[there], att[t].reshape(COLS, width), preferred_element_type=F32)

        for there in range(4):

            @pl.when(there != my_set)
            def _():
                k = (there - my_set + 4) % 4
                part[t, k] = product(there).astype(BF)
                m_copy(t, k).start()

        return product(my_set)

    def finish(t, mixed):
        for k in (1, 3, 2):
            m_copy(t, k).wait_recv()
            mixed = mixed + parts_in[t, k].astype(F32)
        out_ref[:, span(t)] = (resid[:, span(t)].astype(F32) + gcol[...] * mixed).astype(BF)

    def share_weights():

        def share(k):
            quarter_copy(k).wait_recv()
            for d in (2, 1, 3):
                x_copy(k, d).start()

        share(2)

        @pl.when(c == 1)
        def _():
            share(1)
            share(3)

    def await_weights():

        @pl.when(c == 0)
        def _():
            for k in (1, 3):
                for i in range(4):
                    w_copy(k, i).wait_recv()

        @pl.when(c == 1)
        def _():
            for k in (1, 3):
                for d in (1, 3, 2):
                    x_copy(k, d).wait_recv()

        for d in (1, 3, 2):
            x_copy(2, d).wait_recv()

    visit(0, first)
    visit(0, second)
    visit(1, second[::-1])
    visit(1, first)
    share_weights()
    merge(0)
    merge(1)
    await_weights()
    own_parts = [project(t) for t in range(splits)]
    for t in range(splits):
        finish(t, own_parts[t])

    for copy in kv:
        copy.wait_send()
    for t in range(splits):
        for o in range(1, GROUP):
            q_copy(t, o).wait_send()
            p_copy(t, o).wait_send()
        for k in range(1, 8):
            a_copy(t, k).wait_send()
        for k in range(1, 4):
            m_copy(t, k).wait_send()
    def drain(k):
        quarter_copy(k).wait_send()
        for d in range(1, 4):
            x_copy(k, d).wait_send()

    drain(2)

    @pl.when(c == 0)
    def _():
        for k in (1, 3):
            for i in range(4):
                w_copy(k, i).wait_send()

    @pl.when(c == 1)
    def _():
        drain(1)
        drain(3)


def local(splits, q, lk, lv, ck, cv, windows, *args):
    width = TOK // splits
    hbm = pl.BlockSpec(memory_space=pltpu.HBM)
    dma = pltpu.SemaphoreType.DMA
    return pl.pallas_call(
        functools.partial(kernel, splits),
        out_shape=jax.ShapeDtypeStruct((FEAT, TOK), BF),
        in_specs=[hbm] * 12,
        out_specs=pl.BlockSpec(memory_space=pltpu.VMEM),
        scratch_shapes=[
            pltpu.VMEM((GROUP, TOK, HEAD), BF),
            pltpu.VMEM((4, FRAME, HEAD), BF),
            pltpu.VMEM((4, FRAME, HEAD), BF),
            pltpu.VMEM((4, HEAD, FRAME), BF),
            pltpu.VMEM((TOK, HEAD), BF),
            pltpu.VMEM((TOK, HEAD), BF),
            pltpu.VMEM((HEAD, TOK), BF),
            pltpu.VMEM((splits, GROUP, MSG, width), BF),
            pltpu.VMEM((splits, GROUP, MSG, width), BF),
            pltpu.VMEM((splits, 8, HEAD, width), BF),
            pltpu.VMEM((4, FEAT, COLS), BF),
            pltpu.VMEM((splits, 4, FEAT, width), BF),
            pltpu.VMEM((splits, 4, FEAT, width), BF),
            pltpu.VMEM((FEAT, TOK), BF),
            pltpu.VMEM((50, FEAT), F32),
            pltpu.VMEM((FEAT, 1), F32),
            pltpu.SMEM((4, 16), jnp.int32),
            pltpu.SMEM((16,), jnp.int32),
            pltpu.SMEM((32,), jnp.int32),
            pltpu.SMEM((1,), jnp.int32),
            dma((15,)),
            dma((2,)), dma((2,)),
            dma((splits, GROUP)), dma((splits, GROUP)),
            dma((splits, GROUP)), dma((splits, GROUP)),
            dma((splits, 8)), dma((splits, 8)),
            dma((4, NZH)), dma((4, NZH)),
            dma((splits, 4)), dma((splits, 4)),
        ],
        compiler_params=pltpu.CompilerParams(
            collective_id=0, has_side_effects=True, vmem_limit_bytes=60 << 20
        ),
        name="block_attention_projection",
    )(q, lk, lv, ck, cv, windows.T, *args)


def solution(mesh):
    return jax.shard_map(
        functools.partial(local, 2),
        mesh=mesh,
        in_specs=(
            P("frames", "heads"),
            P("frames", "heads"),
            P("frames", "heads"),
            P("frames", None, "heads"),
            P("frames", None, "heads"),
            P(),
            P(),
            P(),
            P("heads", "frames"),
            P("heads", None),
            P(None, "heads"),
            P(),
        ),
        out_specs=P("heads", "frames"),
        check_vma=False,
    )
```

```python
import functools

import jax
import jax.numpy as jnp
from jax import lax
from jax.experimental import pallas as pl
from jax.experimental.pallas import tpu as pltpu
from jax.sharding import PartitionSpec as P

MESH = pl.DeviceIdType.MESH
BF = jnp.bfloat16
F32 = jnp.float32
NX, NZL, NC, NZH, NY = 4, 2, 2, 4, 8
GROUP = NX * NZL
HEAD = 128
TOK = 256
FRAME = 512
FEAT = 160
COLS = 8 * HEAD
MSG = HEAD + 16
NEG = -(2.0**100)
SCALE2 = HEAD ** (-0.5) * 1.4426950408889634


def coords():
    f = lax.axis_index("frames")
    h = lax.axis_index("heads")
    return f // 8, (f // 2) % 4, f % 2, h // 8, h % 8


def device(zl, x, c, zh, y):
    return (zl * 8 + x * 2 + c, zh * 8 + y)


def kernel(
    splits,
    q_hbm, lk_hbm, lv_hbm, ck_hbm, cv_hbm, windows_hbm, counts_hbm, slots_hbm, res_hbm, w_hbm, gate_hbm, step_hbm,
    out_hbm,
    qall, kbuf, vbuf, vt, lk, lv, lvt, sent, came, att, wg, part, parts_in, resid, gate, gcol, updated,
    windows, counts, slot_of, step,
    sem_load, sem_out, sem_kv_s, sem_kv_r, sem_q_s, sem_q_r, sem_p_s, sem_p_r,
    sem_a_s, sem_a_r, sem_w_s, sem_w_r, sem_m_s, sem_m_r,
):
    zl, x, c, zh, y = coords()
    width = TOK // splits
    even = 1 - c
    pair, side = y // 2, y % 2
    my_set = even * pair + c * zh
    my_slot = even * (2 * zh + side) + c * y

    def frame_peer(o, sign):
        dz, dx = o // NX, o % NX
        return device((zl + dz) % NZL, (x + sign * dx + NX) % NX, c, zh, y)

    def set_peer(k):
        slot = (my_slot + k) % 8
        return device(zl, x, c, even * (slot // 2) + c * zh, even * (2 * pair + slot % 2) + c * slot)

    def feature_peer(k):
        there = (my_set + k) % 4
        return device(zl, x, c, even * zh + c * there, even * (2 * there + side) + c * y)

    def columns(there, i):
        start = (even * i + c * there) * 1024 + (even * there + c * i) * 256
        return pl.ds(pl.multiple_of(start, 256), 256)

    other_core = device(zl, x, 1 - c, zh, y)

    mine = pl.ds(pl.multiple_of(c * 2, 2), 2)
    near = [
        (ck_hbm, kbuf.at[mine]), (cv_hbm, vbuf.at[mine]), (q_hbm, qall.at[0]), (lk_hbm, lk), (lv_hbm, lv),
        (windows_hbm, windows), (counts_hbm, counts), (slots_hbm, slot_of), (step_hbm, step), (gate_hbm, gate),
        (res_hbm, resid),
    ]
    for i in range(4):
        near.append((w_hbm.at[:, columns(my_set, i)], wg.at[my_set, :, pl.ds(i * 256, 256)]))
    loads = [pltpu.make_async_copy(src, dst, sem_load.at[i]) for i, (src, dst) in enumerate(near)]
    barrier = pltpu.get_barrier_semaphore()
    peers = [frame_peer(o, 1) for o in range(1, GROUP)]
    peers += [other_core]
    peers += [set_peer(k) for k in range(1, 8)]
    peers += [feature_peer(k) for k in range(1, 4)]
    for peer in peers:
        pl.semaphore_signal(barrier, inc=1, device_id=peer, device_id_type=MESH)
    early, late = loads[:9], loads[9:]
    for load in early:
        load.start()
    pl.semaphore_wait(barrier, len(peers))

    def remote(src, dst, send, recv, peer):
        return pltpu.make_async_remote_copy(
            src_ref=src, dst_ref=dst, send_sem=send, recv_sem=recv, device_id=peer, device_id_type=MESH
        )

    def span(t):
        return pl.ds(t * width, width)

    kv = [
        remote(ck_hbm, kbuf.at[mine], sem_kv_s.at[0], sem_kv_r.at[0], other_core),
        remote(cv_hbm, vbuf.at[mine], sem_kv_s.at[1], sem_kv_r.at[1], other_core),
    ]

    def q_copy(t, o):
        return remote(
            q_hbm.at[span(t)], qall.at[o, span(t)], sem_q_s.at[t, o], sem_q_r.at[t, o], frame_peer(o, 1)
        )

    def p_copy(t, o):
        return remote(sent.at[t, o], came.at[t, o], sem_p_s.at[t, o], sem_p_r.at[t, o], frame_peer(o, -1))

    def a_copy(t, k):
        here = att.at[t, my_slot]
        return remote(here, here, sem_a_s.at[t, k], sem_a_r.at[t, k], set_peer(k))

    def w_copy(k, i):
        return remote(
            w_hbm.at[:, columns((my_set + k) % 4, i)],
            wg.at[my_set, :, pl.ds(i * 256, 256)], sem_w_s.at[k, i], sem_w_r.at[k, i], feature_peer(k),
        )

    def quarter_copy(k):
        return remote(
            w_hbm.at[:, columns((my_set + k) % 4, x)],
            wg.at[my_set, :, pl.ds(pl.multiple_of(x * 256, 256), 256)],
            sem_w_s.at[k, 0], sem_w_r.at[k, 0], feature_peer(k),
        )

    def x_copy(k, d):
        block = wg.at[(my_set + 4 - k) % 4, :, pl.ds(pl.multiple_of(x * 256, 256), 256)]
        return remote(block, block, sem_w_s.at[k, d], sem_w_r.at[k, d], frame_peer(d, 1))

    def m_copy(t, k):
        return remote(part.at[t, k], parts_in.at[t, k], sem_m_s.at[t, k], sem_m_r.at[t, k], feature_peer(k))

    for copy in kv:
        copy.start()
    first, second = [0, 1, 4, 3], [5, 7, 2, 6]
    orders = (first + second, second[::-1] + first)
    for t in range(splits):
        for o in orders[t]:
            if o > 0:
                q_copy(t, o).start()
    for load in late:
        load.start()
    for load in early:
        load.wait()

    quarter_copy(2).start()

    @pl.when(c == 0)
    def _():
        for k in (1, 3):
            for i in range(4):
                w_copy(k, i).start()

    @pl.when(c == 1)
    def _():
        for k in (1, 3):
            quarter_copy(k).start()

    lvt[...] = lv[...].T
    for i in range(2):
        vt[c * 2 + i] = vbuf[c * 2 + i].T
    for copy in kv:
        copy.wait_recv()
    for i in range(2):
        vt[(1 - c) * 2 + i] = vbuf[(1 - c) * 2 + i].T

    def listed(block, holder):
        frame, live = 0, 0
        for j in range(4):
            slot = slot_of[windows[j, block]]
            hit = jnp.logical_and(j < counts[block], slot // 2 == holder).astype(jnp.int32)
            frame = frame + hit * (slot % 2)
            live = live + hit
        return frame, live

    def scores(keys, q):
        return lax.dot_general(keys, q, (((1,), (1,)), ((), ())), preferred_element_type=F32)

    def attend(t, offsets):
        units = []
        for o in offsets:
            q = qall[o, span(t)]
            dz, dx = o // NX, o % NX
            block = ((zl + dz) % NZL) * 8 + ((x - dx + NX) % NX) * 2 + c
            pieces = []
            for d in range(2):
                frame, live = listed(block, zl * 8 + x * 2 + d)
                pieces.append((scores(kbuf[2 * d + frame], q), jnp.full((1, width), live, jnp.int32) > 0, vt.at[2 * d + frame]))
            if o == 0:
                pieces.append((scores(lk[...], q), None, lvt))
            units.append(pieces)
        results = []
        for pieces in units:
            tops = []
            for s, on, _ in pieces:
                top = jnp.max(s, axis=0, keepdims=True) * SCALE2
                tops.append(top if on is None else jnp.where(on, top, NEG))
            m = functools.reduce(jnp.maximum, tops).astype(BF).astype(F32)
            total, result = 0.0, 0.0
            for s, on, values in pieces:
                p = jnp.exp2(s * SCALE2 + (-m if on is None else jnp.where(on, -m, NEG)))
                total = total + jnp.sum(p, axis=0, keepdims=True)
                result = result + jnp.dot(values[...], p.astype(BF), preferred_element_type=F32)
            results.append((m, total, result))
        return results

    def visit(t, offsets):
        for o in offsets:
            if o > 0:
                q_copy(t, o).wait_recv()
        for o, (m, total, result) in zip(offsets, attend(t, offsets)):
            high = total.astype(BF).astype(F32)
            row = lax.broadcasted_iota(jnp.int32, (16, width), 0)
            stats = jnp.where(row == 0, m, jnp.where(row == 1, high, total - high))
            sent[t, o, 0:HEAD] = result.astype(BF)
            sent[t, o, HEAD:MSG] = stats.astype(BF)
            if o > 0:
                p_copy(t, o).start()

    def merge(t):
        for o in range(1, GROUP):
            p_copy(t, o).wait_recv()
        stats = [(sent if o == 0 else came)[t, o, HEAD:MSG].astype(F32) for o in range(GROUP)]
        m = functools.reduce(jnp.maximum, [each[0:1] for each in stats])
        total, result = 0.0, 0.0
        for o in range(GROUP):
            share = jnp.exp2(stats[o][0:1] - m)
            total = total + share * (stats[o][1:2] + stats[o][2:3])
            result = result + share * (sent if o == 0 else came)[t, o, 0:HEAD].astype(F32)
        att[t, my_slot] = (result / total).astype(BF)
        for slot in range(8):

            @pl.when(slot != my_slot)
            def _():
                a_copy(t, (slot - my_slot + 8) % 8).start()

    def project(t):
        for k in range(1, 8):
            a_copy(t, k).wait_recv()

        def product(there):
            return jnp.dot(wg[there], att[t].reshape(COLS, width), preferred_element_type=F32)

        for there in range(4):

            @pl.when(there != my_set)
            def _():
                k = (there - my_set + 4) % 4
                part[t, k] = product(there).astype(BF)
                m_copy(t, k).start()

        return product(my_set)

    def finish(t, mixed):
        for k in (1, 3, 2):
            m_copy(t, k).wait_recv()
            mixed = mixed + parts_in[t, k].astype(F32)
        updated[:, span(t)] = (resid[:, span(t)].astype(F32) + gcol[...] * mixed).astype(BF)

    def share_weights():

        def share(k):
            quarter_copy(k).wait_recv()
            for d in (2, 1, 3):
                x_copy(k, d).start()

        share(2)

        @pl.when(c == 1)
        def _():
            share(1)
            share(3)

    def await_weights():

        @pl.when(c == 0)
        def _():
            for k in (1, 3):
                for i in range(4):
                    w_copy(k, i).wait_recv()

        @pl.when(c == 1)
        def _():
            for k in (1, 3):
                for d in (1, 3, 2):
                    x_copy(k, d).wait_recv()

        for d in (1, 3, 2):
            x_copy(2, d).wait_recv()

    visit(0, first)
    visit(0, second)
    visit(1, second[::-1])
    visit(1, first)
    share_weights()
    for load in late:
        load.wait()
    hot = lax.broadcasted_iota(jnp.int32, gate.shape, 0) == step[0]
    gcol[...] = jnp.sum(jnp.where(hot, gate[...], 0.0).T, axis=1, keepdims=True)
    merge(0)
    merge(1)
    await_weights()
    own_parts = [project(t) for t in range(splits)]
    outs = [
        pltpu.make_async_copy(updated.at[:, span(t)], out_hbm.at[:, span(t)], sem_out.at[t]) for t in range(splits)
    ]
    for t in range(splits):
        finish(t, own_parts[t])
        outs[t].start()

    for copy in kv:
        copy.wait_send()
    for t in range(splits):
        for o in range(1, GROUP):
            q_copy(t, o).wait_send()
            p_copy(t, o).wait_send()
        for k in range(1, 8):
            a_copy(t, k).wait_send()
        for k in range(1, 4):
            m_copy(t, k).wait_send()
    def drain(k):
        quarter_copy(k).wait_send()
        for d in range(1, 4):
            x_copy(k, d).wait_send()

    drain(2)
    for out in outs:
        out.wait()

    @pl.when(c == 0)
    def _():
        for k in (1, 3):
            for i in range(4):
                w_copy(k, i).wait_send()

    @pl.when(c == 1)
    def _():
        drain(1)
        drain(3)


def local(splits, q, lk, lv, ck, cv, windows, *args):
    width = TOK // splits
    hbm = pl.BlockSpec(memory_space=pltpu.HBM)
    dma = pltpu.SemaphoreType.DMA
    return pl.pallas_call(
        functools.partial(kernel, splits),
        out_shape=jax.ShapeDtypeStruct((FEAT, TOK), BF),
        in_specs=[hbm] * 12,
        out_specs=hbm,
        scratch_shapes=[
            pltpu.VMEM((GROUP, TOK, HEAD), BF),
            pltpu.VMEM((4, FRAME, HEAD), BF),
            pltpu.VMEM((4, FRAME, HEAD), BF),
            pltpu.VMEM((4, HEAD, FRAME), BF),
            pltpu.VMEM((TOK, HEAD), BF),
            pltpu.VMEM((TOK, HEAD), BF),
            pltpu.VMEM((HEAD, TOK), BF),
            pltpu.VMEM((splits, GROUP, MSG, width), BF),
            pltpu.VMEM((splits, GROUP, MSG, width), BF),
            pltpu.VMEM((splits, 8, HEAD, width), BF),
            pltpu.VMEM((4, FEAT, COLS), BF),
            pltpu.VMEM((splits, 4, FEAT, width), BF),
            pltpu.VMEM((splits, 4, FEAT, width), BF),
            pltpu.VMEM((FEAT, TOK), BF),
            pltpu.VMEM((50, FEAT), F32),
            pltpu.VMEM((FEAT, 1), F32),
            pltpu.VMEM((FEAT, TOK), BF),
            pltpu.SMEM((4, 16), jnp.int32),
            pltpu.SMEM((16,), jnp.int32),
            pltpu.SMEM((32,), jnp.int32),
            pltpu.SMEM((1,), jnp.int32),
            dma((15,)),
            dma((splits,)),
            dma((2,)), dma((2,)),
            dma((splits, GROUP)), dma((splits, GROUP)),
            dma((splits, GROUP)), dma((splits, GROUP)),
            dma((splits, 8)), dma((splits, 8)),
            dma((4, NZH)), dma((4, NZH)),
            dma((splits, 4)), dma((splits, 4)),
        ],
        compiler_params=pltpu.CompilerParams(
            collective_id=0, has_side_effects=True, vmem_limit_bytes=60 << 20
        ),
        name="block_attention_projection",
    )(q, lk, lv, ck, cv, windows.T, *args)


def solution(mesh):
    return jax.shard_map(
        functools.partial(local, 2),
        mesh=mesh,
        in_specs=(
            P("frames", "heads"),
            P("frames", "heads"),
            P("frames", "heads"),
            P("frames", None, "heads"),
            P("frames", None, "heads"),
            P(),
            P(),
            P(),
            P("heads", "frames"),
            P("heads", None),
            P(None, "heads"),
            P(),
        ),
        out_specs=P("heads", "frames"),
        check_vma=False,
    )
```
